32 devices in a mesh: roll: 16 (over z, y, x), tp: 2 (over core).
Axes of the slice: x: 2, y: 2, z: 4, core: 2. Of those that a mesh axis runs over, the one named last changes fastest.
Arguments:
- hidden_rows: bfloat16 [12288, 7168], P('roll', 'tp'), may hold values from -100 to 100
- target_latents: bfloat16 [12288, 576], P('roll'), may hold values from -6 to 6
- group_lengths: int32 [16, 8], P('roll'), may hold values from 1 to 288, 768 in all within a row
- dest_ids: int32 [12288, 1], P('roll'), may hold values from 0 to 15; in each aligned block of 768 rows (0 to 767, 768 to 1535, ...) at most 72 rows name the same one
- input_gain: float32 [7168], P('tp'), may hold values from 0.1 to 1.9
- latent_gain: float32 [512], replicated, may hold values from 0.1 to 1.9
- kv_weight: bfloat16 [7168, 576], P('tp'), may hold values from -0.0625 to 0.0625
Outputs:
- trainer_loss: float32 [16], P('roll')
- weight_codes: bfloat16 [7168, 576], P('tp')
The draws below stay inside these ranges and needn't reach their ends.
Inputs may be any that keep to these rules, and one draw needn't show every extreme that they name: `dest_ids`: at most 72 of the rows of one index of roll name the same trainer, and exactly 72 in some index. `group_lengths`: each index's 8 lengths sum to 768; the longest is exactly 288.
All inputs are finite; a program needn't handle non-finite values. Where the reference program divides by a largest or mean magnitude, that divisor is 1e-20 or more.
Results may differ from the reference program's by a relative error of at most 0.0085.
Values may be sent and summed in bfloat16 or wider, within the bound.
No kernel may reach another device: no remote copies, remote signals or barrier semaphores. Data moves between devices by JAX's collectives and lax.ppermute only.
A program may use at most 128 MiB of HBM per device.

```python
import math
import jax
import jax.numpy as jnp
import numpy as np
from jax import lax

D = 7168
LAT = 512
KVW = 576
SRC_DEV = 768
GROUPS = 8
ROWS = 12288
CAP = 72
N_ROLL = 16


def draw_hidden_rows(key, part):
    key = jax.random.fold_in(key, 11)
    key_body, key_rows = jax.random.split(key, 2)
    column = jnp.arange(D, dtype=jnp.float32) / D
    column_scale = jnp.power(10.0, column)[None, :]
    row_scale = jnp.exp(jax.random.uniform(key_rows, (ROWS, 1), jnp.float32, 0.0, math.log(10.0)))
    values = jax.random.truncated_normal(key_body, -4.0, 4.0, (ROWS, D), jnp.float32) * row_scale * column_scale * 0.25
    return values.astype(jnp.bfloat16)


def level_of(own_key, dims, pieces, smallest, largest):
    def one(dim, shards_of):
        heights = jax.random.uniform(jax.random.fold_in(jax.random.fold_in(own_key, 6), dim), (shards_of,), jnp.float32, smallest / len(pieces), largest / len(pieces))
        return jnp.repeat(jnp.exp(heights), dims[dim] // shards_of).reshape((-1,) + (1,) * (len(dims) - dim - 1))

    factor_of = one(*pieces[0])
    for cut in pieces[1:]:
        factor_of = factor_of * one(*cut)
    return factor_of


def split_up(number_of, total, most, skew):
    loads = [(1 << 20) // math.isqrt(grade ** skew) + 1 for grade in range(2, number_of + 1)]
    surplus, given = total - most - (number_of - 1), [1] * (number_of - 1)
    while surplus > 0:
        movable = [i for i in range(number_of - 1) if given[i] < most]
        mass, left = sum([loads[i] for i in movable]), surplus
        for i in movable:
            more = min(most - given[i], max(1, left * loads[i] // mass), surplus)
            given[i] = given[i] + more
            surplus = surplus - more
    return np.array([most] + given)


def ragged_sizes(rng, amount, total, reach, skew):
    if amount == 2:
        one = jax.random.randint(rng, (), max(1, total - reach), min(reach, total - 1) + 1)
        return jnp.stack([one, total - one])
    sizes = jnp.asarray(split_up(amount, total, reach, skew), jnp.int32)
    couples = (amount - 1) // 2
    donor, sink = sizes[1:1 + 2 * couples:2], sizes[2:2 + 2 * couples:2]
    room = jnp.minimum(donor - 1, reach - sink)
    shifted = jax.random.randint(jax.random.fold_in(rng, 1), (couples,), 0, 1 << 20) % (room + 1)
    sizes = sizes.at[1:1 + 2 * couples:2].set(donor - shifted).at[2:2 + 2 * couples:2].set(sink + shifted)
    return sizes[jax.random.permutation(jax.random.fold_in(rng, 2), amount)]


def assign_block(own_key, own, number, rows, amount, top, reach, skew):
    order = jax.random.permutation(own_key, amount)
    crowded, usual = portions_of(amount, rows * top, reach, skew, True), portions_of(amount, rows * top, reach, skew, False)
    places = jnp.arange(amount)

    def named(sizes, rotation):
        used = int((sizes > 0).sum())
        fixed = max(1, used // 4)
        moved = fixed + (places - fixed + rotation * (used - fixed)) % max(1, amount - fixed)
        return jnp.zeros((amount,), jnp.int32).at[order[jnp.where(places < fixed, places, moved)]].set(jnp.asarray(sizes, jnp.int32))

    sizes = jnp.where(number % 4 == 0, named(crowded, number // 4), named(usual, number - number // 4 - 1))
    mixed = jax.random.permutation(jax.random.fold_in(own, 3), amount)
    donor, taker = mixed[0:amount // 2 * 2:2], mixed[1:amount // 2 * 2:2]
    margin = jnp.minimum(sizes[donor] - 1, reach - sizes[taker]) // 2
    margin = jnp.where((donor == order[0]) | (taker == order[0]) | (sizes[taker] == 0), 0, jnp.maximum(margin, 0))
    moved = jax.random.randint(jax.random.fold_in(own, 4), (amount // 2,), 0, 1 << 20) % (margin + 1)
    sizes = sizes.at[donor].add(-moved).at[taker].add(moved)
    members = jnp.searchsorted(jnp.cumsum(sizes), jnp.arange(rows * top), side="right").astype(jnp.int32)
    listing = members.reshape(top, rows).T
    listing = listing[jax.random.permutation(jax.random.fold_in(own, 1), rows)]
    rotation = jax.random.randint(jax.random.fold_in(own, 2), (rows, 1), 0, top)
    return jnp.take_along_axis(listing, (jnp.arange(top)[None, :] + rotation) % top, axis=1)


def portions_of(amount, total, limit, lean, full):
    loads = [(1 << 20) // math.isqrt(rank ** lean) + 1 for rank in range(1, amount + 1)]
    largest = limit if full else min(limit, max(-(-total // amount), total * loads[0] // sum(loads)))
    least = 1 if total - largest >= amount - 1 else 0
    holding, surplus = [largest] + [least] * (amount - 1), total - largest - least * (amount - 1)
    while surplus > 0:
        candidates = [i for i in range(1, amount) if holding[i] < largest] or [i for i in range(1, amount) if holding[i] < limit]
        pool, remaining = sum([loads[i] for i in candidates]), surplus
        for i in candidates:
            more = min(limit - holding[i], max(1, remaining * loads[i] // pool), surplus)
            holding[i] = holding[i] + more
            surplus = surplus - more
    return np.array(holding)


def normal_values(rng, shape, spread, reach, pieces=(), kind=jnp.bfloat16):
    values = jax.random.normal(rng, shape, jnp.float32) * spread
    if len(pieces) > 0:
        values = level_of(rng, shape, pieces, -0.22, 0.18) * values
    return jnp.clip(values, min=-reach, max=reach).astype(kind)


def setup_inputs(seed: int = 0) -> dict:
    keys = jax.random.split(jax.random.key(seed), 8)
    hidden_rows = draw_hidden_rows(jax.random.fold_in(keys[7], 71), 0)
    target_latents = normal_values(keys[1], (ROWS, KVW), 1.0, 6.0, ((0, 16),))
    group_lengths = jax.vmap(lambda own: ragged_sizes(own, GROUPS, SRC_DEV, 3 * SRC_DEV // GROUPS, 2))(jax.random.split(keys[2], N_ROLL)).reshape((N_ROLL, GROUPS)).astype(jnp.int32)
    dest_ids_keys = jax.random.split(jax.random.fold_in(keys[3], 1), ROWS // SRC_DEV)
    dest_ids_turns = jax.random.permutation(jax.random.fold_in(keys[3], 3), ROWS // SRC_DEV)
    dest_ids = jax.vmap(lambda own, number: assign_block(jax.random.fold_in(keys[3], 2), own, number, SRC_DEV, ROWS // SRC_DEV, 1, CAP, 2))(dest_ids_keys, dest_ids_turns).reshape((ROWS, 1))
    input_gain = jnp.clip(1.0 + 0.18 * jax.random.normal(keys[4], (D,), jnp.float32), 0.1, 1.9)
    latent_gain = jnp.clip(1.0 + 0.18 * jax.random.normal(keys[5], (LAT,), jnp.float32), 0.1, 1.9)
    kv_weight = normal_values(keys[6], (D, KVW), D ** -0.5, 0.0625, ((0, 2),))
    return dict(hidden_rows=hidden_rows, target_latents=target_latents, group_lengths=group_lengths, dest_ids=dest_ids, input_gain=input_gain, latent_gain=latent_gain, kv_weight=kv_weight)


EPS = 1e-06
RATE = 0.5

def row_weights(lengths, row_count):
    bounds = jnp.cumsum(lengths)
    position = jnp.arange(row_count, dtype=jnp.int32)
    group_index = lax.optimization_barrier(jnp.sum((position[:, None] >= bounds[None, :]).astype(jnp.int32), axis=1))
    member = group_index[:, None] == jnp.arange(lengths.shape[0], dtype=jnp.int32)[None, :]
    length = lax.optimization_barrier(jnp.sum(jnp.where(member, lengths[None, :], 0), axis=1))
    return (1.0 / length.astype(jnp.float32)).astype(jnp.bfloat16)

def head_terms(latent, targets, weights, gain_vec, groups):
    latent_width = gain_vec.shape[0]
    compressed = latent[:, :latent_width]
    rotary = latent[:, latent_width:]
    factor = lax.rsqrt(lax.optimization_barrier(jnp.mean(compressed * compressed, axis=1)) + EPS)
    predicted = compressed * factor[:, None] * gain_vec
    weight_f = weights.astype(jnp.float32)
    residue = jnp.concatenate([predicted, rotary], axis=1) - targets.astype(jnp.float32)
    row_terms = weight_f * (0.5 * lax.optimization_barrier(jnp.mean(residue * residue, axis=1))) / groups
    d_pred = weight_f[:, None] * residue
    d_scaled = d_pred[:, :latent_width] * gain_vec
    inner_sum = lax.optimization_barrier(jnp.mean(d_scaled * compressed, axis=1))
    d_compressed = factor[:, None] * d_scaled - compressed * (factor * factor * factor * inner_sum)[:, None]
    return (row_terms, jnp.concatenate([d_compressed, d_pred[:, latent_width:]], axis=1))

def reference(hidden_rows, target_latents, group_lengths, dest_ids, input_gain, latent_gain, kv_weight):
    weights_all = jax.vmap(lambda lengths: row_weights(lengths, SRC_DEV))(group_lengths)
    blocks_x = hidden_rows.reshape(N_ROLL, SRC_DEV, D)
    blocks_t = target_latents.reshape(N_ROLL, SRC_DEV, KVW)
    blocks_d = dest_ids.reshape(N_ROLL, SRC_DEV)

    def step_block(carry, items):
        grad_acc, loss_acc = carry
        rows_x, rows_t, rows_w, rows_d = items
        wide = rows_x.astype(jnp.float32)
        scale = lax.rsqrt(lax.optimization_barrier(jnp.mean(wide * wide, axis=1)) + EPS)
        normed = (wide * scale[:, None] * input_gain).astype(jnp.bfloat16)
        latent = jnp.dot(normed, kv_weight, preferred_element_type=jnp.float32)
        row_terms, d_latent = head_terms(latent, rows_t, rows_w, latent_gain, GROUPS)
        grad_acc = grad_acc + jnp.dot(normed.T, d_latent.astype(jnp.bfloat16), preferred_element_type=jnp.float32)
        loss_acc = loss_acc + jax.ops.segment_sum(row_terms, rows_d, num_segments=N_ROLL)
        return ((grad_acc, loss_acc), None)
    start = (jnp.zeros((D, KVW), jnp.float32), jnp.zeros((N_ROLL,), jnp.float32))
    (grad, trainer_loss), _ = lax.scan(step_block, start, (blocks_x, blocks_t, weights_all, blocks_d))
    power = jnp.mean(grad * grad)
    updated = kv_weight.astype(jnp.float32) - RATE * grad * lax.rsqrt(power + EPS)
    peak = lax.optimization_barrier(jnp.max(jnp.abs(updated), axis=0)) + EPS
    weight_codes = (updated / peak[None, :]).astype(jnp.bfloat16)
    return (trainer_loss, weight_codes)
```

```python
import jax
import jax.numpy as jnp
from jax import lax
from jax.experimental import pallas as pl
from jax.experimental.pallas import tpu as pltpu
from jax.sharding import PartitionSpec as P

EPS = 1e-06
RATE = 0.5
F32 = jnp.float32
BF16 = jnp.bfloat16

STEPS = {"xy": (1, 2), "yx": (2, 1), "z_lo": (4, 4), "z_hi": (8, 8)}
ROW_ORDER = ("xy", "yx", "z_lo", "z_hi")
COL_ORDER = ("z_lo", "xy", "yx", "z_hi")


def row_weights(lengths, row_count):
    bounds = jnp.cumsum(lengths)
    position = lax.iota(jnp.int32, row_count)
    group_index = jnp.sum((position[None, :] >= bounds[:, None]).astype(jnp.int32), axis=0)
    member = group_index[None, :] == lax.iota(jnp.int32, lengths.shape[0])[:, None]
    length = jnp.sum(jnp.where(member, lengths[:, None], 0), axis=0)
    return (1.0 / length.astype(F32)).astype(BF16)


def exchange(value, step):
    pairs = []
    for roll in range(16):
        for core in range(2):
            pairs.append((2 * roll + core, 2 * (roll ^ STEPS[step][core]) + core))
    return lax.ppermute(value, ("roll", "tp"), pairs)


def swap_cores(value):
    return lax.ppermute(value, "tp", [(0, 1), (1, 0)])


def add(a, b):
    return (a.astype(F32) + b.astype(F32)).astype(a.dtype)


def scatter_step(value, step):
    half = value.shape[0] // 2
    got = exchange(value[half:], step)
    return add(value[:half], got)


def gather_step(value, step):
    return jnp.concatenate([value, exchange(value, step)], axis=0)


def head(latent, targets, weights, gain_vec, groups):
    width = gain_vec.shape[0]
    compressed = latent[:width]
    factor = lax.rsqrt(jnp.mean(compressed * compressed, axis=0) + EPS)
    gain_col = gain_vec[:, None]
    weight_f = weights.astype(F32)
    targets = targets.astype(F32)
    res_c = compressed * factor[None, :] * gain_col - targets[:width]
    res_r = latent[width:] - targets[width:]
    total = jnp.sum(res_c * res_c, axis=0) + jnp.sum(res_r * res_r, axis=0)
    row_terms = weight_f * (0.5 * total / latent.shape[0]) / groups
    scaled = weight_f[None, :] * res_c * gain_col
    inner = jnp.mean(scaled * compressed, axis=0)
    d_c = factor[None, :] * scaled - compressed * (factor * factor * factor * inner)[None, :]
    return row_terms, jnp.concatenate([d_c, weight_f[None, :] * res_r], axis=0)


def update_of(w, g, gain, coef):
    return w.astype(F32) - coef * gain * g.astype(F32)


def peak_kernel(where_ref, coef_ref, g_ref, w_ref, gain_ref, out_ref):
    rows, cols = w_ref.shape[-2:]
    upd = jnp.abs(update_of(w_ref[...].reshape(rows, cols), g_ref[...].reshape(rows, cols), gain_ref[...], coef_ref[0]))
    top = jnp.max(upd, axis=1, keepdims=True)
    out_ref[...] = jnp.broadcast_to(top, (rows, 128)).reshape(out_ref.shape)


def code_kernel(where_ref, coef_ref, g_ref, w_ref, gain_ref, peak_ref, *rest):
    out_ref = rest[-1]
    rows, cols = w_ref.shape[-2:]
    upd = update_of(w_ref[...].reshape(rows, cols), g_ref[...].reshape(rows, cols), gain_ref[...], coef_ref[0])
    inv = 1.0 / peak_ref[...].reshape(rows, 128)[:, :1]
    out_ref[...] = (upd * inv).astype(BF16).reshape(out_ref.shape)


def finish(g_rows, g_cols, w3, gain_row, coef, where):
    blk, feat = w3.shape[1:]
    half = feat // 2
    nr = g_rows.shape[0]
    nc = g_cols.shape[1]
    scal = coef.reshape(1)
    smem = pl.BlockSpec(memory_space=pltpu.SMEM)

    def specs_rows(kern, extra, out_w, outs, alias):
        return pl.pallas_call(
            kern,
            grid_spec=pltpu.PrefetchScalarGridSpec(
                num_scalar_prefetch=1,
                grid=(nr,),
                in_specs=[
                    smem,
                    pl.BlockSpec((1, blk, feat), lambda j, wh: (j ^ wh[0], 0, 0)),
                    pl.BlockSpec((1, blk, feat), lambda j, wh: (j, 0, 0)),
                    pl.BlockSpec((1, feat), lambda j, wh: (0, 0)),
                ]
                + extra,
                out_specs=pl.BlockSpec((1, blk, out_w), lambda j, wh: (j, 0, 0)),
            ),
            out_shape=outs,
            input_output_aliases=alias,
        )

    def specs_cols(kern, extra, out_spec, outs, alias):
        return pl.pallas_call(
            kern,
            grid_spec=pltpu.PrefetchScalarGridSpec(
                num_scalar_prefetch=1,
                grid=(nc, 2),
                in_specs=[
                    smem,
                    pl.BlockSpec((1, 1, blk, half), lambda j, c, wh: (c ^ wh[1], j ^ wh[2], 0, 0)),
                    pl.BlockSpec((1, blk, half), lambda j, c, wh: (nr + j, 0, c)),
                    pl.BlockSpec((1, half), lambda j, c, wh: (0, c)),
                ]
                + extra,
                out_specs=out_spec,
            ),
            out_shape=outs,
            input_output_aliases=alias,
        )

    top_r = specs_rows(peak_kernel, [], 128, jax.ShapeDtypeStruct((nr, blk, 128), F32), {})(
        where, scal, g_rows, w3, gain_row
    )
    top_c = specs_cols(
        peak_kernel,
        [],
        pl.BlockSpec((1, 1, blk, 128), lambda j, c, wh: (c, j, 0, 0)),
        jax.ShapeDtypeStruct((2, nc, blk, 128), F32),
        {},
    )(where, scal, g_cols, w3, gain_row)
    top = jnp.concatenate([top_r, jnp.maximum(top_c[0], top_c[1])], axis=0)
    peak = jnp.maximum(top, swap_cores(top)) + EPS
    shape = jax.ShapeDtypeStruct(w3.shape, BF16)
    part = specs_rows(
        code_kernel, [pl.BlockSpec((1, blk, 128), lambda j, wh: (j, 0, 0))], feat, shape, {}
    )(where, scal, g_rows, w3, gain_row, peak)
    return specs_cols(
        code_kernel,
        [
            pl.BlockSpec((1, blk, 128), lambda j, c, wh: (nr + j, 0, 0)),
            pl.BlockSpec(memory_space=pl.ANY),
        ],
        pl.BlockSpec((1, blk, half), lambda j, c, wh: (nr + j, 0, c)),
        shape,
        {6: 0},
    )(where, scal, g_cols, w3, gain_row, peak, part)


def paired_shards(hidden, targets, group_lengths, dest_ids, input_gain, latent_gain, kv_weight):
    rows, feat = hidden.shape
    width = kv_weight.shape[1]
    model_width = 2 * feat
    groups = group_lengths.shape[1]
    roll = lax.axis_index("roll")
    core = lax.axis_index("tp")
    x_bit, y_bit, lo_bit, hi_bit = roll & 1, (roll >> 1) & 1, (roll >> 2) & 1, (roll >> 3) & 1
    first = jnp.where(core == 0, x_bit, y_bit)
    second = jnp.where(core == 0, y_bit, x_bit)
    row_mask = first * 8 + second * 4 + lo_bit * 2 + hi_bit
    col_mask = first * 4 + second * 2 + hi_bit
    where = jnp.stack([row_mask, lo_bit, col_mask]).astype(jnp.int32)

    w_t = kv_weight.T
    gained = (w_t.astype(F32) * input_gain[None, :]).astype(BF16)
    part = lax.dot_general(gained, hidden, (((1,), (1,)), ((), ())), preferred_element_type=F32)
    wide = hidden.astype(F32)
    squares = jnp.sum(wide * wide, axis=1)
    other = swap_cores(part.astype(BF16))
    squares = squares + swap_cores(squares)
    scale = lax.rsqrt(squares / model_width + EPS)
    latent = (part + other.astype(F32)) * scale[None, :]
    row_terms, d_latent = head(latent, targets.T, row_weights(group_lengths[0], rows), latent_gain, groups)
    d_scaled = (d_latent * scale[None, :]).astype(BF16)
    dest = dest_ids[:, 0]
    losses = jnp.sum(jnp.where(dest[None, :] == lax.iota(jnp.int32, 16)[:, None], row_terms[None, :], 0.0), axis=1)

    blk = width // 24
    d3 = d_scaled.reshape(24, blk, rows)
    d_rows = jnp.take(d3[:16], lax.iota(jnp.int32, 16) ^ row_mask, axis=0)
    d_cols = jnp.take(d3[16:], lax.iota(jnp.int32, 8) ^ col_mask, axis=0)
    half = feat // 2
    g_rows = jnp.dot(d_rows.reshape(16 * blk, rows), hidden, preferred_element_type=F32)
    g_rows = g_rows.astype(BF16).reshape(16, blk, feat)
    g_cols = jnp.dot(d_cols.reshape(8 * blk, rows), hidden, preferred_element_type=F32).astype(BF16)
    g_cols = g_cols.reshape(8, blk, feat)
    left, right = g_cols[:, :, :half], g_cols[:, :, half:]
    swap = lo_bit == 1
    g_cols = jnp.stack([jnp.where(swap, right, left), jnp.where(swap, left, right)])

    for step_r, step_c in zip(ROW_ORDER, COL_ORDER):
        g_rows = scatter_step(g_rows, step_r)
        if g_cols.ndim == 4:
            g_cols = scatter_step(g_cols, step_c)[0]
        else:
            g_cols = scatter_step(g_cols, step_c)

    gain_half = lax.dynamic_slice(input_gain, (lo_bit * half,), (half,))
    own_r = g_rows.astype(F32) * input_gain
    own_c = g_cols.astype(F32) * gain_half
    power = jnp.sum(own_r * own_r) + jnp.sum(own_c * own_c)
    small = jnp.concatenate([0.5 * losses, power[None], jnp.zeros((111,), F32)]).reshape(1, 128)
    for step in ROW_ORDER:
        small = small + exchange(small, step)
    small = small + swap_cores(small)

    for step_r, step_c in zip(reversed(ROW_ORDER), reversed(COL_ORDER)):
        g_rows = gather_step(g_rows, step_r)
        if step_c == "z_lo":
            g_cols = g_cols[None]
        g_cols = gather_step(g_cols, step_c)

    coef = RATE * lax.rsqrt(small[0, 16] / (model_width * width) + EPS)
    codes = finish(g_rows, g_cols, w_t.reshape(24, blk, feat), input_gain[None, :], coef, where)
    loss = lax.dynamic_slice(small, (0, roll), (1, 1))
    return loss.reshape(1), codes.reshape(width, feat).T


def any_shards(hidden, targets, group_lengths, dest_ids, input_gain, latent_gain, kv_weight):
    rows, feat = hidden.shape
    width = kv_weight.shape[1]
    roll_count = lax.axis_size("roll")
    model_width = feat * lax.axis_size("tp")
    wide = hidden.astype(F32)
    scale = lax.rsqrt(lax.psum(jnp.sum(wide * wide, axis=1), "tp") / model_width + EPS)
    normed = (wide * scale[:, None] * input_gain).astype(BF16)
    latent = lax.psum(jnp.dot(normed, kv_weight, preferred_element_type=F32), "tp")
    weights = row_weights(group_lengths[0], rows)
    row_terms, d_latent = head(latent.T, targets.T, weights, latent_gain, group_lengths.shape[1])
    grad = lax.dot_general(
        d_latent.astype(BF16), normed, (((1,), (0,)), ((), ())), preferred_element_type=F32
    )
    grad = lax.psum(grad.astype(BF16), "roll").astype(F32)
    dest = dest_ids[:, 0]
    named = dest[None, :] == lax.iota(jnp.int32, roll_count)[:, None]
    losses = lax.psum(jnp.sum(jnp.where(named, row_terms[None, :], 0.0), axis=1), "roll")
    power = lax.psum(jnp.sum(grad * grad), "tp")
    updated = kv_weight.T.astype(F32) - RATE * grad * lax.rsqrt(power / (model_width * width) + EPS)
    peak = lax.pmax(jnp.max(jnp.abs(updated), axis=1), "tp") + EPS
    codes = (updated / peak[:, None]).astype(BF16)
    loss = lax.dynamic_slice(losses, (lax.axis_index("roll"),), (1,))
    return loss, codes.T


def solution(mesh):
    in_specs = (
        P("roll", "tp"),
        P("roll", None),
        P("roll", None),
        P("roll", None),
        P("tp"),
        P(),
        P("tp", None),
    )
    out_specs = (P("roll"), P("tp", None))
    paired = mesh.shape["roll"] == 16 and mesh.shape["tp"] == 2
    body = paired_shards if paired else any_shards
    return jax.shard_map(body, mesh=mesh, in_specs=in_specs, out_specs=out_specs, check_vma=False)
```

```python
import functools

import jax
import jax.numpy as jnp
from jax import lax
from jax.experimental import pallas as pl
from jax.experimental.pallas import tpu as pltpu
from jax.sharding import PartitionSpec as P

EPS = 1e-06
RATE = 0.5
F32 = jnp.float32
BF16 = jnp.bfloat16

STEPS = {"xy": (1, 2), "yx": (2, 1), "lo": (4, 4), "hi": (8, 8)}

SCATTER = (("xy", "yx", "hi", "lo"), ("xy", "lo", "yx", "hi"), ("lo", "xy", "yx", "hi"))
GATHER = ((3, 2, 1, 0), (3, 2, 0, 1), (3, 2, 0, 1))


def row_weights(lengths, row_count):
    bounds = jnp.cumsum(lengths)
    position = lax.iota(jnp.int32, row_count)
    group_index = jnp.sum((position[None, :] >= bounds[:, None]).astype(jnp.int32), axis=0)
    member = group_index[None, :] == lax.iota(jnp.int32, lengths.shape[0])[:, None]
    length = jnp.sum(jnp.where(member, lengths[:, None], 0), axis=0)
    return (1.0 / length.astype(F32)).astype(BF16)


def exchange(value, step):
    pairs = []
    for roll in range(16):
        for core in range(2):
            pairs.append((2 * roll + core, 2 * (roll ^ STEPS[step][core]) + core))
    return lax.ppermute(value, ("roll", "tp"), pairs)


def swap_cores(value):
    return lax.ppermute(value, "tp", [(0, 1), (1, 0)])


def add(a, b):
    return (a.astype(F32) + b.astype(F32)).astype(a.dtype)


def head(latent, targets, weights, gain_vec, groups):
    width = gain_vec.shape[0]
    compressed = latent[:width]
    factor = lax.rsqrt(jnp.mean(compressed * compressed, axis=0) + EPS)
    gain_col = gain_vec[:, None]
    weight_f = weights.astype(F32)
    targets = targets.astype(F32)
    res_c = compressed * factor[None, :] * gain_col - targets[:width]
    res_r = latent[width:] - targets[width:]
    total = jnp.sum(res_c * res_c, axis=0) + jnp.sum(res_r * res_r, axis=0)
    row_terms = weight_f * (0.5 * total / latent.shape[0]) / groups
    scaled = weight_f[None, :] * res_c * gain_col
    inner = jnp.mean(scaled * compressed, axis=0)
    d_c = factor[None, :] * scaled - compressed * (factor * factor * factor * inner)[None, :]
    return row_terms, jnp.concatenate([d_c, weight_f[None, :] * res_r], axis=0)


def forward_kernel(x_ref, w_ref, gain_ref, part_ref, sent_ref, sq_ref, sq_acc):
    step = pl.program_id(0)
    x = x_ref[...]
    gained = (w_ref[...].astype(F32) * gain_ref[...]).astype(BF16)
    part = lax.dot_general(gained, x, (((1,), (1,)), ((), ())), preferred_element_type=F32)
    wide = x.astype(F32)
    wide = wide * wide
    sq = wide[:, :128]
    for c in range(1, x.shape[1] // 128):
        sq = sq + wide[:, c * 128 : (c + 1) * 128]

    @pl.when(step == 0)
    def _():
        part_ref[...] = part
        sq_acc[...] = sq

    @pl.when(step > 0)
    def _():
        part_ref[...] += part
        sq_acc[...] += sq

    @pl.when(step == pl.num_programs(0) - 1)
    def _():
        ones = jnp.ones((8, 128), F32)
        total = lax.dot_general(
            ones, sq_acc[...], (((1,), (1,)), ((), ())), preferred_element_type=F32, precision=lax.Precision.HIGHEST
        )
        sq_ref[...] = total
        width = part_ref.shape[0]
        sent_ref[:width] = part_ref[...].astype(BF16)
        row = total[:1]
        top = row.astype(BF16)
        rest = row - top.astype(F32)
        mid = rest.astype(BF16)
        low = (rest - mid.astype(F32)).astype(BF16)
        index = lax.broadcasted_iota(jnp.int32, (16, row.shape[1]), 0)
        terms = jnp.where(
            index == 0,
            top.astype(F32),
            jnp.where(index == 1, mid.astype(F32), jnp.where(index == 2, low.astype(F32), 0.0)),
        )
        sent_ref[width:] = terms.astype(BF16)


def forward(x, w_t, gain_row):
    rows, feat = x.shape
    width = w_t.shape[0]
    cols = 512
    return pl.pallas_call(
        forward_kernel,
        grid=(feat // cols,),
        in_specs=[
            pl.BlockSpec((rows, cols), lambda k: (0, k)),
            pl.BlockSpec((width, cols), lambda k: (0, k)),
            pl.BlockSpec((1, cols), lambda k: (0, k)),
        ],
        out_specs=[
            pl.BlockSpec((width, rows), lambda k: (0, 0)),
            pl.BlockSpec((width + 16, rows), lambda k: (0, 0)),
            pl.BlockSpec((8, rows), lambda k: (0, 0)),
        ],
        out_shape=[
            jax.ShapeDtypeStruct((width, rows), F32),
            jax.ShapeDtypeStruct((width + 16, rows), BF16),
            jax.ShapeDtypeStruct((8, rows), F32),
        ],
        scratch_shapes=[pltpu.VMEM((rows, 128), F32)],
        compiler_params=pltpu.CompilerParams(vmem_limit_bytes=24 * 1024 * 1024),
        cost_estimate=pl.CostEstimate(flops=2 * rows * feat * width, bytes_accessed=10_000_000, transcendentals=0),
    )(x, w_t, gain_row)


def head_kernel(model_width, masks_ref, lens_ref, part_ref, got_ref, sq_ref, target_ref, dest_ref, gain_ref, d_ref, loss_ref):
    step = pl.program_id(0)
    width, lanes = part_ref.shape
    lat = gain_ref.shape[0]
    groups = lens_ref.shape[0]
    terms = got_ref[width:].astype(F32)
    squares = sq_ref[:1] + (terms[0:1] + terms[1:2] + terms[2:3])
    scale = lax.rsqrt(squares / model_width + EPS)
    position = lax.broadcasted_iota(jnp.int32, (1, lanes), 1) + step * lanes
    length = jnp.zeros((1, lanes), jnp.int32)
    start = 0
    for g in range(groups):
        size = lens_ref[g]
        length = jnp.where((position >= start) & (position < start + size), size, length)
        start = start + size
    weight = (1.0 / length.astype(F32)).astype(BF16).astype(F32)

    gain = gain_ref[...]
    comp = (part_ref[:lat] + got_ref[:lat].astype(F32)) * scale
    factor = lax.rsqrt(jnp.mean(comp * comp, axis=0, keepdims=True) + EPS)
    res_c = comp * factor * gain - target_ref[:lat].astype(F32)
    res_r = (part_ref[lat:] + got_ref[lat:width].astype(F32)) * scale - target_ref[lat:].astype(F32)
    total = jnp.sum(res_c * res_c, axis=0, keepdims=True) + jnp.sum(res_r * res_r, axis=0, keepdims=True)
    row_terms = weight * (0.5 * (total / width)) / groups
    scaled = weight * res_c * gain
    inner = jnp.mean(scaled * comp, axis=0, keepdims=True)
    d_c = (factor * scale) * scaled - comp * (factor * factor * factor * inner * scale)
    d_r = (weight * scale) * res_r

    blk = d_ref.shape[1]
    for j in range(d_ref.shape[0]):
        lo, hi = j * blk, (j + 1) * blk
        if hi <= lat:
            piece = d_c[lo:hi]
        elif lo >= lat:
            piece = d_r[lo - lat : hi - lat]
        else:
            piece = jnp.concatenate([d_c[lo:], d_r[: hi - lat]], axis=0)
        d_ref[(j // 4) * 4 + ((j % 4) ^ masks_ref[j // 4])] = piece.astype(BF16)

    trainers = loss_ref.shape[0]
    named = dest_ref[...] == lax.broadcasted_iota(jnp.int32, (trainers, lanes), 0)
    sums = jnp.sum(jnp.where(named, row_terms, 0.0), axis=1, keepdims=True)
    sums = jnp.broadcast_to(sums, loss_ref.shape)

    @pl.when(step == 0)
    def _():
        loss_ref[...] = sums

    @pl.when(step > 0)
    def _():
        loss_ref[...] += sums


def head_call(part, got, sq, targets_t, dest_row, lengths, gain_col, row_masks, model_width, trainers):
    width, rows = part.shape
    lanes = 256
    smem = pl.BlockSpec(memory_space=pltpu.SMEM)
    return pl.pallas_call(
        functools.partial(head_kernel, model_width),
        grid=(rows // lanes,),
        in_specs=[
            smem,
            smem,
            pl.BlockSpec((width, lanes), lambda i: (0, i)),
            pl.BlockSpec((width + 16, lanes), lambda i: (0, i)),
            pl.BlockSpec((8, lanes), lambda i: (0, i)),
            pl.BlockSpec((width, lanes), lambda i: (0, i)),
            pl.BlockSpec((1, lanes), lambda i: (0, i)),
            pl.BlockSpec(gain_col.shape, lambda i: (0, 0)),
        ],
        out_specs=[
            pl.BlockSpec((12, width // 12, lanes), lambda i: (0, 0, i)),
            pl.BlockSpec((trainers, 128), lambda i: (0, 0)),
        ],
        out_shape=[
            jax.ShapeDtypeStruct((12, width // 12, rows), BF16),
            jax.ShapeDtypeStruct((trainers, 128), F32),
        ],
        compiler_params=pltpu.CompilerParams(vmem_limit_bytes=24 * 1024 * 1024),
        cost_estimate=pl.CostEstimate(flops=20 * width * rows, bytes_accessed=4_000_000, transcendentals=0),
    )(row_masks, lengths, part, got, sq, targets_t, dest_row, gain_col)


def grad_kernel(first, count, where_ref, d_ref, x_ref, *out_refs):
    blocks, blk, rows = d_ref.shape
    lhs = d_ref[first * 4 : (first + count) * 4].reshape(count * 4 * blk, rows)
    out = jnp.dot(lhs, x_ref[...], preferred_element_type=F32).astype(BF16)
    for c in range(count):
        part = out[c * 4 * blk : (c + 1) * 4 * blk]
        out_refs[c][...] = part.reshape(out_refs[c].shape)


def grad_half(first, count, d, x, half, low_masks):
    rows, feat = x.shape
    cols = feat // 4
    blk = d.shape[1]
    where = jnp.stack([half, *low_masks]).astype(jnp.int32)
    return pl.pallas_call(
        functools.partial(grad_kernel, first, count),
        grid_spec=pltpu.PrefetchScalarGridSpec(
            num_scalar_prefetch=1,
            grid=(2,),
            in_specs=[
                pl.BlockSpec(d.shape, lambda i, wh: (0, 0, 0)),
                pl.BlockSpec((rows, cols), lambda i, wh: (0, wh[0] * 2 + i)),
            ],
            out_specs=[
                pl.BlockSpec((1, 4, blk, cols), lambda i, wh, c=c: (i ^ wh[1 + c], 0, 0, 0)) for c in range(count)
            ],
        ),
        out_shape=[jax.ShapeDtypeStruct((2, 4, blk, cols), BF16)] * count,
        compiler_params=pltpu.CompilerParams(vmem_limit_bytes=24 * 1024 * 1024),
        cost_estimate=pl.CostEstimate(
            flops=2 * count * 4 * blk * rows * feat // 2, bytes_accessed=rows * feat, transcendentals=0
        ),
    )(where, d, x)


def code_kernel(where_ref, coef_ref, g_ref, w_ref, gain_ref, peak_ref, *rest):
    out_ref = rest[-1]
    blk = g_ref.shape[2]
    factor = coef_ref[0] * gain_ref[...]
    for j in range(4):
        rows = slice(j * blk, (j + 1) * blk)
        g = g_ref[0, j ^ where_ref[2]].astype(F32)
        inv = 1.0 / peak_ref[rows, :1]
        out_ref[rows] = ((w_ref[rows].astype(F32) - factor * g) * inv).astype(BF16)


def code_piece(chain, piece, w_t, gain_row, coef, peak, columns, row_mask, codes):
    blk, cols = piece.shape[-2:]
    piece = piece.reshape(2, 4, blk, cols)
    where = jnp.stack([*columns, row_mask]).astype(jnp.int32)
    extra = [] if codes is None else [codes]
    return pl.pallas_call(
        code_kernel,
        grid_spec=pltpu.PrefetchScalarGridSpec(
            num_scalar_prefetch=1,
            grid=(2,),
            in_specs=[
                pl.BlockSpec(memory_space=pltpu.SMEM),
                pl.BlockSpec((1, 4, blk, cols), lambda i, wh: (i, 0, 0, 0)),
                pl.BlockSpec((4 * blk, cols), lambda i, wh: (chain, wh[i])),
                pl.BlockSpec((1, cols), lambda i, wh: (0, wh[i])),
                pl.BlockSpec((4 * blk, 128), lambda i, wh: (chain, 0)),
            ]
            + [pl.BlockSpec(memory_space=pl.ANY)] * len(extra),
            out_specs=pl.BlockSpec((4 * blk, cols), lambda i, wh: (chain, wh[i])),
        ),
        out_shape=jax.ShapeDtypeStruct(w_t.shape, BF16),
        input_output_aliases={6: 0} if extra else {},
        compiler_params=pltpu.CompilerParams(vmem_limit_bytes=24 * 1024 * 1024),
        cost_estimate=pl.CostEstimate(flops=16 * blk * cols, bytes_accessed=48 * blk * cols, transcendentals=0),
    )(where, coef, piece, w_t, gain_row, peak, *extra)


def paired_shards(hidden, targets, group_lengths, dest_ids, input_gain, latent_gain, kv_weight):
    rows, feat = hidden.shape
    width = kv_weight.shape[1]
    model_width = 2 * feat
    blk, cols = width // 12, feat // 4
    roll = lax.axis_index("roll")
    core = lax.axis_index("tp")
    x_bit, y_bit = roll & 1, (roll >> 1) & 1
    bit = {
        "xy": jnp.where(core == 0, x_bit, y_bit),
        "yx": jnp.where(core == 0, y_bit, x_bit),
        "lo": (roll >> 2) & 1,
        "hi": (roll >> 3) & 1,
    }
    bits = [[bit[step] for step in order] for order in SCATTER]
    row_masks = [b[2] * 2 + b[3] for b in bits]

    w_t = kv_weight.T
    gain_row = input_gain[None, :]
    part, sent, squares = forward(hidden, w_t, gain_row)
    got = swap_cores(sent)
    d, losses = head_call(
        part,
        got,
        squares,
        targets.T,
        dest_ids.T,
        group_lengths[0],
        latent_gain[:, None],
        jnp.stack(row_masks).astype(jnp.int32),
        model_width,
        16,
    )

    out_a, out_b = grad_half(0, 2, d, hidden, 1 - bits[0][0], [bits[0][1], bits[1][1]])
    (out_c,) = grad_half(2, 1, d, hidden, 1 - bits[2][0], [bits[2][1]])
    in_a, in_b = grad_half(0, 2, d, hidden, bits[0][0], [bits[0][1], bits[1][1]])
    (in_c,) = grad_half(2, 1, d, hidden, bits[2][0], [bits[2][1]])
    shape = (2, 2, 2, blk, cols)
    sums = []
    for order, away, keep in zip(SCATTER, (out_a, out_b, out_c), (in_a, in_b, in_c)):
        value = add(keep.reshape(shape), exchange(away.reshape(shape), order[0]))
        for step in order[1:]:
            value = add(value[0], exchange(value[1], step))
        sums.append(value)

    own_cols = [b[0] * 2 + b[1] for b in bits]
    own_gain = [lax.dynamic_slice(gain_row, (0, c * cols), (1, cols)) for c in own_cols]
    power = sum(jnp.sum(jnp.square(v.astype(F32) * g)) for v, g in zip(sums, own_gain))
    small = jnp.concatenate([0.5 * losses, jnp.broadcast_to(power, (8, 128))], axis=0)
    for step in ("xy", "yx", "lo", "hi"):
        small = small + exchange(small, step)
    small = small + swap_cores(small)
    coef = RATE * lax.rsqrt(small[16, :1] / (model_width * width) + EPS)

    peak = jnp.zeros((3, 4, blk), F32)
    for chain in range(3):
        own_w = lax.dynamic_slice(
            w_t, (chain * 4 * blk + row_masks[chain] * blk, own_cols[chain] * cols), (blk, cols)
        )
        updated = own_w.astype(F32) - coef * own_gain[chain] * sums[chain].astype(F32)
        top = jnp.max(jnp.abs(updated), axis=1)
        peak = lax.dynamic_update_slice(peak, top[None, None], (chain, row_masks[chain], 0))
    for step in ("xy", "yx", "lo", "hi"):
        peak = jnp.maximum(peak, exchange(peak, step))
    peak = jnp.maximum(peak, swap_cores(peak)) + EPS
    peak = jnp.broadcast_to(peak.reshape(width, 1), (width, 128))

    pieces = []
    for chain in range(3):
        value = sums[chain].reshape(1, 1, 1, 1, blk, cols)
        for axis in GATHER[chain][:3]:
            value = jnp.concatenate([value, exchange(value, SCATTER[chain][axis])], axis=axis)
        pieces.append((value, exchange(value, SCATTER[chain][GATHER[chain][3]])))

    codes = None
    for p in range(2):
        for chain in (2, 1, 0):
            last = GATHER[chain][3]
            mine = own_cols[chain]
            columns = [(2 * p + i if last == 0 else 2 * i + p) ^ mine for i in range(2)]
            codes = code_piece(
                chain, pieces[chain][p], w_t, gain_row, coef, peak, columns, row_masks[chain], codes
            )
    loss = lax.dynamic_slice(small, (roll, 0), (1, 1))
    return loss.reshape(1), codes.T


def any_shards(hidden, targets, group_lengths, dest_ids, input_gain, latent_gain, kv_weight):
    rows, feat = hidden.shape
    width = kv_weight.shape[1]
    roll_count = lax.axis_size("roll")
    model_width = feat * lax.axis_size("tp")
    wide = hidden.astype(F32)
    scale = lax.rsqrt(lax.psum(jnp.sum(wide * wide, axis=1), "tp") / model_width + EPS)
    normed = (wide * scale[:, None] * input_gain).astype(BF16)
    latent = lax.psum(jnp.dot(normed, kv_weight, preferred_element_type=F32), "tp")
    weights = row_weights(group_lengths[0], rows)
    row_terms, d_latent = head(latent.T, targets.T, weights, latent_gain, group_lengths.shape[1])
    grad = lax.dot_general(
        d_latent.astype(BF16), normed, (((1,), (0,)), ((), ())), preferred_element_type=F32
    )
    grad = lax.psum(grad.astype(BF16), "roll").astype(F32)
    dest = dest_ids[:, 0]
    named = dest[None, :] == lax.iota(jnp.int32, roll_count)[:, None]
    losses = lax.psum(jnp.sum(jnp.where(named, row_terms[None, :], 0.0), axis=1), "roll")
    power = lax.psum(jnp.sum(grad * grad), "tp")
    updated = kv_weight.T.astype(F32) - RATE * grad * lax.rsqrt(power / (model_width * width) + EPS)
    peak = lax.pmax(jnp.max(jnp.abs(updated), axis=1), "tp") + EPS
    codes = (updated / peak[:, None]).astype(BF16)
    loss = lax.dynamic_slice(losses, (lax.axis_index("roll"),), (1,))
    return loss, codes.T


def solution(mesh):
    in_specs = (
        P("roll", "tp"),
        P("roll", None),
        P("roll", None),
        P("roll", None),
        P("tp"),
        P(),
        P("tp", None),
    )
    out_specs = (P("roll"), P("tp", None))
    paired = mesh.shape["roll"] == 16 and mesh.shape["tp"] == 2
    body = paired_shards if paired else any_shards
    return jax.shard_map(body, mesh=mesh, in_specs=in_specs, out_specs=out_specs, check_vma=False)
```

```python
import functools

import jax
import jax.numpy as jnp
from jax import lax
from jax.experimental import pallas as pl
from jax.experimental.pallas import tpu as pltpu
from jax.sharding import PartitionSpec as P

EPS = 1e-06
RATE = 0.5
F32 = jnp.float32
BF16 = jnp.bfloat16

STEPS = {"xy": (1, 2), "yx": (2, 1), "lo": (4, 4), "hi": (8, 8)}

SCATTER = (("xy", "yx", "hi", "lo"), ("xy", "lo", "yx", "hi"), ("lo", "xy", "yx", "hi"))
GATHER = ((3, 2, 1, 0), (3, 2, 0, 1), (3, 0, 2, 1))
PLAN = (0, 2, 1, 0, 0, 1, 2, 1, 2, 0, 0, 2, 2, 1, 1, 2, 2, 0, 1, 0, 1, 2, 2, 0, 0, 1, 1, 2, 0, 0, 2, 1, 1, 3, 1, 1, 3, 3, 2, 2, 0, 3, 1, 0, 3, 1, 2, 2, 3, 3, 0, 3, 3, 0, 3, 1, 0, 2)
SMALL = ("xy", "yx", "lo", "hi")


def row_weights(lengths, row_count):
    bounds = jnp.cumsum(lengths)
    position = lax.iota(jnp.int32, row_count)
    group_index = jnp.sum((position[None, :] >= bounds[:, None]).astype(jnp.int32), axis=0)
    member = group_index[None, :] == lax.iota(jnp.int32, lengths.shape[0])[:, None]
    length = jnp.sum(jnp.where(member, lengths[:, None], 0), axis=0)
    return (1.0 / length.astype(F32)).astype(BF16)


def exchange(value, step):
    pairs = []
    for roll in range(16):
        for core in range(2):
            pairs.append((2 * roll + core, 2 * (roll ^ STEPS[step][core]) + core))
    return lax.ppermute(value, ("roll", "tp"), pairs)


def swap_cores(value):
    return lax.ppermute(value, "tp", [(0, 1), (1, 0)])


def add(a, b):
    return (a.astype(F32) + b.astype(F32)).astype(a.dtype)


def head(latent, targets, weights, gain_vec, groups):
    width = gain_vec.shape[0]
    compressed = latent[:width]
    factor = lax.rsqrt(jnp.mean(compressed * compressed, axis=0) + EPS)
    gain_col = gain_vec[:, None]
    weight_f = weights.astype(F32)
    targets = targets.astype(F32)
    res_c = compressed * factor[None, :] * gain_col - targets[:width]
    res_r = latent[width:] - targets[width:]
    total = jnp.sum(res_c * res_c, axis=0) + jnp.sum(res_r * res_r, axis=0)
    row_terms = weight_f * (0.5 * total / latent.shape[0]) / groups
    scaled = weight_f[None, :] * res_c * gain_col
    inner = jnp.mean(scaled * compressed, axis=0)
    d_c = factor[None, :] * scaled - compressed * (factor * factor * factor * inner)[None, :]
    return row_terms, jnp.concatenate([d_c, weight_f[None, :] * res_r], axis=0)


def forward_kernel(
    chunks, x_hbm, w_hbm, gain_ref, part_ref, sent_ref, sq_ref, x_ref, w_ref, sems
):
    rows, feat = x_ref.shape
    width = w_ref.shape[0]
    cols = feat // chunks
    copies = []
    for k in range(chunks):
        span = slice(k * cols, (k + 1) * cols)
        pairs = ((w_hbm, w_ref), (x_hbm, x_ref))
        copies.append(
            [pltpu.make_async_copy(a.at[:, span], b.at[:, span], sems.at[n, k]) for n, (a, b) in enumerate(pairs)]
        )
    for pair in copies:
        for copy in pair:
            copy.start()
    sq = None
    for k in range(chunks):
        span = slice(k * cols, (k + 1) * cols)
        for copy in copies[k]:
            copy.wait()
        gained = (w_ref[:, span].astype(F32) * gain_ref[:, span]).astype(BF16)
        x = x_ref[:, span]
        part = lax.dot_general(gained, x, (((1,), (1,)), ((), ())), preferred_element_type=F32)
        if k > 0:
            part = part + part_ref[...]
        part_ref[...] = part
        if k == chunks - 1:
            sent_ref[:width] = part.astype(BF16)
        wide = x.astype(F32)
        wide = wide * wide
        for c in range(cols // 128):
            piece = wide[:, c * 128 : (c + 1) * 128]
            sq = piece if sq is None else sq + piece
    total = lax.dot_general(
        jnp.ones((8, 128), F32), sq, (((1,), (1,)), ((), ())), preferred_element_type=F32, precision=lax.Precision.HIGHEST
    )
    sq_ref[...] = total
    row = total[:1]
    top = row.astype(BF16)
    rest = row - top.astype(F32)
    mid = rest.astype(BF16)
    low = (rest - mid.astype(F32)).astype(BF16)
    index = lax.broadcasted_iota(jnp.int32, (16, rows), 0)
    terms = jnp.where(
        index == 0,
        top.astype(F32),
        jnp.where(index == 1, mid.astype(F32), jnp.where(index == 2, low.astype(F32), 0.0)),
    )
    sent_ref[width:] = terms.astype(BF16)


def whole():
    return pl.BlockSpec(memory_space=pltpu.VMEM)


def scalars():
    return pl.BlockSpec(memory_space=pltpu.SMEM)


def far():
    return pl.BlockSpec(memory_space=pltpu.HBM)


def in_hbm(value):
    return pltpu.with_memory_space_constraint(value, pltpu.HBM)


def vmem_limit(mib):
    return pltpu.CompilerParams(vmem_limit_bytes=mib * 1024 * 1024)


def forward(x, w_t, gain_row):
    rows, feat = x.shape
    width = w_t.shape[0]
    return pl.pallas_call(
        functools.partial(forward_kernel, 2),
        in_specs=[far(), far(), whole()],
        out_specs=[whole()] * 3,
        out_shape=[
            jax.ShapeDtypeStruct((width, rows), F32),
            jax.ShapeDtypeStruct((width + 16, rows), BF16),
            jax.ShapeDtypeStruct((8, rows), F32),
        ],
        scratch_shapes=[
            pltpu.VMEM(x.shape, BF16),
            pltpu.VMEM(w_t.shape, BF16),
            pltpu.SemaphoreType.DMA((2, 2)),
        ],
        compiler_params=vmem_limit(24),
        cost_estimate=pl.CostEstimate(flops=2 * rows * feat * width, bytes_accessed=10_000_000, transcendentals=0),
    )(in_hbm(x), in_hbm(w_t), gain_row)


def head_kernel(
    model_width,
    where_ref,
    masks_ref,
    lens_ref,
    part_ref,
    got_ref,
    sq_ref,
    t_hbm,
    dest_ref,
    gain_ref,
    x_hbm,
    d_ref,
    loss_ref,
    a_ref,
    b_ref,
    c_ref,
    target_ref,
    x_ref,
    sems,
):
    t_copy = pltpu.make_async_copy(t_hbm, target_ref, sems.at[0])
    x_copy = pltpu.make_async_copy(x_hbm, x_ref, sems.at[1])
    t_copy.start()
    x_copy.start()
    width, rows = part_ref.shape
    lat = gain_ref.shape[0]
    groups = lens_ref.shape[0]
    blk = d_ref.shape[1]
    trainers = loss_ref.shape[0]
    lanes = 256
    gain = gain_ref[...]
    sums = None
    t_copy.wait()
    for first in range(0, rows, lanes):
        cut = slice(first, first + lanes)
        terms = got_ref[width:, cut].astype(F32)
        squares = sq_ref[:1, cut] + (terms[0:1] + terms[1:2] + terms[2:3])
        scale = lax.rsqrt(squares / model_width + EPS)
        position = lax.broadcasted_iota(jnp.int32, (1, lanes), 1) + first
        length = jnp.zeros((1, lanes), jnp.int32)
        start = 0
        for g in range(groups):
            size = lens_ref[g]
            length = jnp.where((position >= start) & (position < start + size), size, length)
            start = start + size
        weight = (1.0 / length.astype(F32)).astype(BF16).astype(F32)

        comp = (part_ref[:lat, cut] + got_ref[:lat, cut].astype(F32)) * scale
        factor = lax.rsqrt(jnp.mean(comp * comp, axis=0, keepdims=True) + EPS)
        res_c = comp * factor * gain - target_ref[:lat, cut].astype(F32)
        res_r = (part_ref[lat:, cut] + got_ref[lat:width, cut].astype(F32)) * scale
        res_r = res_r - target_ref[lat:, cut].astype(F32)
        total = jnp.sum(res_c * res_c, axis=0, keepdims=True) + jnp.sum(res_r * res_r, axis=0, keepdims=True)
        row_terms = weight * (0.5 * (total / width)) / groups
        scaled = weight * res_c * gain
        inner = jnp.mean(scaled * comp, axis=0, keepdims=True)
        d_c = (factor * scale) * scaled - comp * (factor * factor * factor * inner * scale)
        d_r = (weight * scale) * res_r
        for j in range(d_ref.shape[0]):
            lo, hi = j * blk, (j + 1) * blk
            if hi <= lat:
                piece = d_c[lo:hi]
            elif lo >= lat:
                piece = d_r[lo - lat : hi - lat]
            else:
                piece = jnp.concatenate([d_c[lo:], d_r[: hi - lat]], axis=0)
            d_ref[(j // 4) * 4 + ((j % 4) ^ masks_ref[j // 4]), :, cut] = piece.astype(BF16)
        named = dest_ref[:, cut] == lax.broadcasted_iota(jnp.int32, (trainers, lanes), 0)
        named = jnp.where(named, row_terms, 0.0)
        for c in range(0, lanes, 128):
            sums = named[:, c : c + 128] if sums is None else sums + named[:, c : c + 128]
    loss_ref[...] = jnp.broadcast_to(jnp.sum(sums, axis=1, keepdims=True), loss_ref.shape)
    x_copy.wait()
    grad_halves(where_ref, d_ref, x_ref, (a_ref, b_ref, c_ref))


def grad_halves(where_ref, d_ref, x_ref, out_refs):
    blocks, blk, rows = d_ref.shape
    cols = out_refs[0].shape[-1]
    for first, count in ((2, 1), (0, 2)):
        lhs = d_ref[first * 4 : (first + count) * 4].reshape(count * 4 * blk, rows)
        for i in range(2):
            col = pl.multiple_of((where_ref[2 * first] * 2 + i) * cols, 128)
            out = jnp.dot(lhs, x_ref[:, pl.ds(col, cols)], preferred_element_type=F32).astype(BF16)
            for c in range(count):
                part = out[c * 4 * blk : (c + 1) * 4 * blk]
                out_refs[first + c][i ^ where_ref[2 * (first + c) + 1]] = part.reshape(4, blk, cols)


def head_call(part, got, sq, targets_t, dest_row, lengths, gain_col, x, where, row_masks, model_width, trainers):
    width, rows = part.shape
    blk, cols = width // 12, x.shape[1] // 4
    return pl.pallas_call(
        functools.partial(head_kernel, model_width),
        in_specs=[scalars()] * 3 + [whole()] * 3 + [far()] + [whole()] * 2 + [far()],
        out_specs=[whole()] * 5,
        out_shape=[
            jax.ShapeDtypeStruct((12, blk, rows), BF16),
            jax.ShapeDtypeStruct((trainers, 128), F32),
        ]
        + [jax.ShapeDtypeStruct((2, 4, blk, cols), BF16)] * 3,
        scratch_shapes=[
            pltpu.VMEM(targets_t.shape, BF16),
            pltpu.VMEM(x.shape, BF16),
            pltpu.SemaphoreType.DMA((2,)),
        ],
        compiler_params=vmem_limit(24),
        cost_estimate=pl.CostEstimate(flops=width * rows * cols * 4, bytes_accessed=12_000_000, transcendentals=0),
    )(where, row_masks, lengths, part, got, sq, in_hbm(targets_t), dest_row, gain_col, in_hbm(x))


def keep_kernel(where_ref, d_ref, x_hbm, a_ref, b_ref, c_ref, x_ref, sem):
    copy = pltpu.make_async_copy(x_hbm, x_ref, sem)
    copy.start()
    copy.wait()
    grad_halves(where_ref, d_ref, x_ref, (a_ref, b_ref, c_ref))


def keep_call(d, x, where):
    blk, cols = d.shape[1], x.shape[1] // 4
    return pl.pallas_call(
        keep_kernel,
        in_specs=[scalars(), whole(), far()],
        out_specs=[whole()] * 3,
        out_shape=[jax.ShapeDtypeStruct((2, 4, blk, cols), BF16)] * 3,
        scratch_shapes=[pltpu.VMEM(x.shape, BF16), pltpu.SemaphoreType.DMA],
        compiler_params=vmem_limit(24),
        cost_estimate=pl.CostEstimate(flops=12 * blk * d.shape[2] * cols * 4, bytes_accessed=10_000_000, transcendentals=0),
    )(where, d, in_hbm(x))


def w_copies(where_ref, w_hbm, w_buf, sem, count):
    rows, cols = w_buf.shape[1:]
    copies = []
    for s in range(count):
        chain = (s % 6) // 2
        col = pl.multiple_of(where_ref[s] * cols, 128)
        tile = w_hbm.at[pl.ds(chain * rows, rows), pl.ds(col, cols)]
        copies.append(pltpu.make_async_copy(tile, w_buf.at[s], sem.at[s]))
        copies[-1].start()
    return copies


def updated_block(where_ref, coef_ref, gain_ref, w_buf, g_ref, s, j, mask):
    blk, cols = g_ref.shape[2:]
    col = pl.multiple_of(where_ref[s] * cols, 128)
    factor = coef_ref[0] * gain_ref[:, pl.ds(col, cols)]
    g = g_ref[s % 2, j ^ mask].astype(F32)
    return w_buf[s, j * blk : (j + 1) * blk].astype(F32) - factor * g


def top_kernel(where_ref, coef_ref, gain_ref, w_hbm, start_ref, a_ref, b_ref, c_ref, out_ref, w_buf, sem):
    copies = w_copies(where_ref, w_hbm, w_buf, sem, 6)
    blk, cols = a_ref.shape[2:]
    for s in range(6):
        chain = s // 2
        copies[s].wait()
        for j in range(4):
            g_ref = (a_ref, b_ref, c_ref)[chain]
            size = jnp.abs(
                updated_block(where_ref, coef_ref, gain_ref, w_buf, g_ref, s, j, where_ref[6 + chain])
            )
            here = slice((chain * 4 + j) * blk, (chain * 4 + j + 1) * blk)
            top = start_ref[here] if s % 2 == 0 else out_ref[here]
            for k in range(cols // 128):
                top = jnp.maximum(top, size[:, k * 128 : (k + 1) * 128])
            out_ref[here] = top


def top_part(pieces, w_t, gain_row, coef, start, columns, row_masks):
    blk, cols = pieces[0].shape[-2:]
    where = jnp.stack([*columns, *row_masks]).astype(jnp.int32)
    return pl.pallas_call(
        top_kernel,
        in_specs=[scalars(), scalars(), whole(), far()] + [whole()] * 4,
        out_specs=whole(),
        out_shape=jax.ShapeDtypeStruct((w_t.shape[0], 128), F32),
        scratch_shapes=[pltpu.VMEM((6, 4 * blk, cols), BF16), pltpu.SemaphoreType.DMA((6,))],
        compiler_params=vmem_limit(24),
        cost_estimate=pl.CostEstimate(flops=4 * w_t.size, bytes_accessed=2 * w_t.size, transcendentals=0),
    )(where, coef, gain_row, in_hbm(w_t), start, *pieces)


def code_kernel(where_ref, coef_ref, gain_ref, w_hbm, mine_ref, other_ref, *rest):
    g_refs, (out_ref, buf, w_buf, inv_ref, sem, w_sem) = rest[:6], rest[6:]
    loads = w_copies(where_ref, w_hbm, w_buf, w_sem, 12)
    blk, cols = g_refs[0].shape[2:]
    rows = 4 * blk
    top = jnp.max(jnp.maximum(mine_ref[...], other_ref[...]), axis=1, keepdims=True)
    inv_ref[...] = jnp.broadcast_to(1.0 / (top + EPS), inv_ref.shape)
    copies = []
    for s in range(12):
        chain = (s % 6) // 2
        g_ref = g_refs[3 * (s // 6) + chain]
        loads[s].wait()
        for j in range(4):
            new = updated_block(where_ref, coef_ref, gain_ref, w_buf, g_ref, s, j, where_ref[12 + chain])
            first = chain * rows + j * blk
            inv = jnp.concatenate([inv_ref[first : first + blk]] * (cols // 128), axis=1)
            buf[s, j * blk : (j + 1) * blk] = (new * inv).astype(BF16)
        col = pl.multiple_of(where_ref[s] * cols, 128)
        tile = out_ref.at[pl.ds(chain * rows, rows), pl.ds(col, cols)]
        copies.append(pltpu.make_async_copy(buf.at[s], tile, sem.at[s]))
        copies[-1].start()
    for copy in copies:
        copy.wait()


def code_all(pieces, w_t, gain_row, coef, mine, other, columns, row_masks):
    blk, cols = pieces[0].shape[-2:]
    where = jnp.stack([*columns, *row_masks]).astype(jnp.int32)
    return pl.pallas_call(
        code_kernel,
        in_specs=[scalars(), scalars(), whole(), far()] + [whole()] * 8,
        out_specs=far(),
        out_shape=jax.ShapeDtypeStruct(w_t.shape, BF16),
        scratch_shapes=[
            pltpu.VMEM((12, 4 * blk, cols), BF16),
            pltpu.VMEM((12, 4 * blk, cols), BF16),
            pltpu.VMEM((w_t.shape[0], 128), F32),
            pltpu.SemaphoreType.DMA((12,)),
            pltpu.SemaphoreType.DMA((12,)),
        ],
        compiler_params=vmem_limit(24),
        cost_estimate=pl.CostEstimate(flops=8 * w_t.size, bytes_accessed=6 * w_t.size, transcendentals=0),
    )(where, coef, gain_row, in_hbm(w_t), mine, other, *pieces)


def paired_shards(hidden, targets, group_lengths, dest_ids, input_gain, latent_gain, kv_weight):
    rows, feat = hidden.shape
    width = kv_weight.shape[1]
    model_width = 2 * feat
    blk, cols = width // 12, feat // 4
    roll = lax.axis_index("roll")
    core = lax.axis_index("tp")
    x_bit, y_bit = roll & 1, (roll >> 1) & 1
    bit = {
        "xy": jnp.where(core == 0, x_bit, y_bit),
        "yx": jnp.where(core == 0, y_bit, x_bit),
        "lo": (roll >> 2) & 1,
        "hi": (roll >> 3) & 1,
    }
    bits = [[bit[step] for step in order] for order in SCATTER]
    row_masks = [b[2] * 2 + b[3] for b in bits]

    w_t = kv_weight.T
    gain_row = input_gain[None, :]
    part, sent, squares = forward(hidden, w_t, gain_row)
    got = swap_cores(sent)
    give = jnp.stack([v for b in bits for v in (1 - b[0], b[1])]).astype(jnp.int32)
    take = jnp.stack([v for b in bits for v in (b[0], b[1])]).astype(jnp.int32)
    d, losses, *away = head_call(
        part,
        got,
        squares,
        targets.T,
        dest_ids.T,
        group_lengths[0],
        latent_gain[:, None],
        hidden,
        give,
        jnp.stack(row_masks).astype(jnp.int32),
        model_width,
        16,
    )
    held = keep_call(d, hidden, take)
    own_cols = [b[0] * 2 + b[1] for b in bits]
    own_gain = [lax.dynamic_slice(gain_row, (0, c * cols), (1, cols)) for c in own_cols]
    shape = (1, 2, 2, 2, blk, cols)
    away = [v.reshape(shape) for v in away]
    held = [v.reshape(shape) for v in held]
    taken = [0] * 4
    flight = [None] * 4
    sums = [None] * 3
    settled = []
    small = None
    for lane in PLAN:
        step, taken[lane] = divmod(taken[lane], 2)[0], taken[lane] + 1
        if flight[lane] is None:
            if lane == 3:
                if step == 0:
                    power = sum(jnp.sum(jnp.square(v.astype(F32) * g)) for v, g in zip(sums, own_gain))
                    small = jnp.concatenate([0.5 * losses, jnp.broadcast_to(power, (8, 128))], axis=0)
                message = small
            elif step == 0:
                message = away[lane]
            elif step < 4:
                message = lax.index_in_dim(held[lane], 1, step, keepdims=True)
            else:
                message = held[lane]
            if settled:
                message, *_ = lax.optimization_barrier((message, *settled))
                settled = []
            if lane == 3:
                flight[lane] = exchange(message, SMALL[step]) if step < 4 else swap_cores(message)
            else:
                order = SCATTER[lane]
                flight[lane] = exchange(message, order[step] if step < 4 else order[GATHER[lane][step - 4]])
            continue
        got, flight[lane] = flight[lane], None
        if lane == 3:
            small = small + got
            settled.append(small)
        elif step < 4:
            keep = held[lane] if step == 0 else lax.index_in_dim(held[lane], 0, step, keepdims=True)
            held[lane] = sums[lane] = add(keep, got)
            settled.append(held[lane])
        elif step < 7:
            held[lane] = jnp.concatenate([held[lane], got], axis=GATHER[lane][step - 4])
            settled.append(held[lane])
        else:
            held[lane] = (held[lane], got)

    coef = RATE * lax.rsqrt(small[16, :1] / (model_width * width) + EPS)
    top = jnp.zeros((width, 128), F32)
    pieces, columns = [], []
    for n in range(2):
        part = [held[chain][n].reshape(2, 4, blk, cols) for chain in range(3)]
        spots = []
        for chain in range(3):
            inner = GATHER[chain][3] == 1
            spots += [(2 * i + n if inner else 2 * n + i) ^ own_cols[chain] for i in range(2)]
        top = top_part(part, w_t, gain_row, coef, top, spots, row_masks)
        pieces += part
        columns += spots
    codes = code_all(pieces, w_t, gain_row, coef, top, swap_cores(top), columns, row_masks)
    loss = lax.dynamic_slice(small, (roll, 0), (1, 1))
    return loss.reshape(1), codes.T


def any_shards(hidden, targets, group_lengths, dest_ids, input_gain, latent_gain, kv_weight):
    rows, feat = hidden.shape
    width = kv_weight.shape[1]
    roll_count = lax.axis_size("roll")
    model_width = feat * lax.axis_size("tp")
    wide = hidden.astype(F32)
    scale = lax.rsqrt(lax.psum(jnp.sum(wide * wide, axis=1), "tp") / model_width + EPS)
    normed = (wide * scale[:, None] * input_gain).astype(BF16)
    latent = lax.psum(jnp.dot(normed, kv_weight, preferred_element_type=F32), "tp")
    weights = row_weights(group_lengths[0], rows)
    row_terms, d_latent = head(latent.T, targets.T, weights, latent_gain, group_lengths.shape[1])
    grad = lax.dot_general(
        d_latent.astype(BF16), normed, (((1,), (0,)), ((), ())), preferred_element_type=F32
    )
    grad = lax.psum(grad.astype(BF16), "roll").astype(F32)
    dest = dest_ids[:, 0]
    named = dest[None, :] == lax.iota(jnp.int32, roll_count)[:, None]
    losses = lax.psum(jnp.sum(jnp.where(named, row_terms[None, :], 0.0), axis=1), "roll")
    power = lax.psum(jnp.sum(grad * grad), "tp")
    updated = kv_weight.T.astype(F32) - RATE * grad * lax.rsqrt(power / (model_width * width) + EPS)
    peak = lax.pmax(jnp.max(jnp.abs(updated), axis=1), "tp") + EPS
    codes = (updated / peak[:, None]).astype(BF16)
    loss = lax.dynamic_slice(losses, (lax.axis_index("roll"),), (1,))
    return loss, codes.T


def solution(mesh):
    in_specs = (
        P("roll", "tp"),
        P("roll", None),
        P("roll", None),
        P("roll", None),
        P("tp"),
        P(),
        P("tp", None),
    )
    out_specs = (P("roll"), P("tp", None))
    paired = mesh.shape["roll"] == 16 and mesh.shape["tp"] == 2
    body = paired_shards if paired else any_shards
    return jax.shard_map(body, mesh=mesh, in_specs=in_specs, out_specs=out_specs, check_vma=False)
```

```python
import functools

import jax
import jax.numpy as jnp
from jax import lax
from jax.experimental import pallas as pl
from jax.experimental.pallas import tpu as pltpu
from jax.sharding import PartitionSpec as P

EPS = 1e-06
RATE = 0.5
F32 = jnp.float32
BF16 = jnp.bfloat16

STEPS = {"xy": (1, 2), "yx": (2, 1), "lo": (4, 4), "hi": (8, 8)}

SCATTER = (("xy", "yx", "hi", "lo"), ("xy", "lo", "yx", "hi"), ("lo", "xy", "yx", "hi"))
GATHER = ((3, 2, 1, 0), (3, 2, 0, 1), (3, 0, 2, 1))
PLAN = (0, 2, 1, 0, 0, 1, 2, 1, 2, 0, 0, 2, 2, 1, 1, 2, 2, 0, 1, 0, 1, 2, 2, 0, 0, 1, 1, 2, 0, 0, 2, 1, 1, 3, 1, 1, 3, 3, 2, 2, 0, 3, 1, 0, 3, 1, 2, 2, 3, 3, 0, 3, 3, 0, 3, 1, 0, 2)
SMALL = ("xy", "yx", "lo", "hi")


def row_weights(lengths, row_count):
    bounds = jnp.cumsum(lengths)
    position = lax.iota(jnp.int32, row_count)
    group_index = jnp.sum((position[None, :] >= bounds[:, None]).astype(jnp.int32), axis=0)
    member = group_index[None, :] == lax.iota(jnp.int32, lengths.shape[0])[:, None]
    length = jnp.sum(jnp.where(member, lengths[:, None], 0), axis=0)
    return (1.0 / length.astype(F32)).astype(BF16)


def exchange(value, step):
    pairs = []
    for roll in range(16):
        for core in range(2):
            pairs.append((2 * roll + core, 2 * (roll ^ STEPS[step][core]) + core))
    return lax.ppermute(value, ("roll", "tp"), pairs)


def swap_cores(value):
    return lax.ppermute(value, "tp", [(0, 1), (1, 0)])


def add(a, b):
    return (a.astype(F32) + b.astype(F32)).astype(a.dtype)


def head(latent, targets, weights, gain_vec, groups):
    width = gain_vec.shape[0]
    compressed = latent[:width]
    factor = lax.rsqrt(jnp.mean(compressed * compressed, axis=0) + EPS)
    gain_col = gain_vec[:, None]
    weight_f = weights.astype(F32)
    targets = targets.astype(F32)
    res_c = compressed * factor[None, :] * gain_col - targets[:width]
    res_r = latent[width:] - targets[width:]
    total = jnp.sum(res_c * res_c, axis=0) + jnp.sum(res_r * res_r, axis=0)
    row_terms = weight_f * (0.5 * total / latent.shape[0]) / groups
    scaled = weight_f[None, :] * res_c * gain_col
    inner = jnp.mean(scaled * compressed, axis=0)
    d_c = factor[None, :] * scaled - compressed * (factor * factor * factor * inner)[None, :]
    return row_terms, jnp.concatenate([d_c, weight_f[None, :] * res_r], axis=0)


def gain_slice(gain_ref, first, count):
    return jnp.concatenate([gain_ref[pl.ds(first // 128 + c, 1)] for c in range(count // 128)], axis=1)


def forward_kernel(
    chunks, x_hbm, w_hbm, gain_hbm, part_ref, sent_ref, sq_ref, x_ref, w_ref, gain_ref, sems, gain_sem
):
    rows, feat = x_ref.shape
    width = w_ref.shape[0]
    cols = feat // chunks
    copies = []
    for k in range(chunks):
        span = slice(k * cols, (k + 1) * cols)
        pairs = ((w_hbm, w_ref), (x_hbm, x_ref))
        copies.append(
            [pltpu.make_async_copy(a.at[:, span], b.at[:, span], sems.at[n, k]) for n, (a, b) in enumerate(pairs)]
        )
    gains = pltpu.make_async_copy(gain_hbm, gain_ref, gain_sem)
    gains.start()
    for pair in copies:
        for copy in pair:
            copy.start()
    gains.wait()
    sq = None
    for k in range(chunks):
        span = slice(k * cols, (k + 1) * cols)
        for copy in copies[k]:
            copy.wait()
        gained = (w_ref[:, span].astype(F32) * gain_slice(gain_ref, k * cols, cols)).astype(BF16)
        x = x_ref[:, span]
        part = lax.dot_general(gained, x, (((1,), (1,)), ((), ())), preferred_element_type=F32)
        if k > 0:
            part = part + part_ref[...]
        part_ref[...] = part
        if k == chunks - 1:
            sent_ref[:width] = part.astype(BF16)
        wide = x.astype(F32)
        wide = wide * wide
        for c in range(cols // 128):
            piece = wide[:, c * 128 : (c + 1) * 128]
            sq = piece if sq is None else sq + piece
    total = lax.dot_general(
        jnp.ones((8, 128), F32), sq, (((1,), (1,)), ((), ())), preferred_element_type=F32, precision=lax.Precision.HIGHEST
    )
    sq_ref[...] = total
    row = total[:1]
    top = row.astype(BF16)
    rest = row - top.astype(F32)
    mid = rest.astype(BF16)
    low = (rest - mid.astype(F32)).astype(BF16)
    index = lax.broadcasted_iota(jnp.int32, (16, rows), 0)
    terms = jnp.where(
        index == 0,
        top.astype(F32),
        jnp.where(index == 1, mid.astype(F32), jnp.where(index == 2, low.astype(F32), 0.0)),
    )
    sent_ref[width:] = terms.astype(BF16)


def whole():
    return pl.BlockSpec(memory_space=pltpu.VMEM)


def scalars():
    return pl.BlockSpec(memory_space=pltpu.SMEM)


def far():
    return pl.BlockSpec(memory_space=pltpu.HBM)


def in_hbm(value):
    return pltpu.with_memory_space_constraint(value, pltpu.HBM)


def vmem_limit(mib):
    return pltpu.CompilerParams(vmem_limit_bytes=mib * 1024 * 1024)


def forward(x, w_t, gains):
    rows, feat = x.shape
    width = w_t.shape[0]
    return pl.pallas_call(
        functools.partial(forward_kernel, 2),
        in_specs=[far(), far(), far()],
        out_specs=[whole()] * 3,
        out_shape=[
            jax.ShapeDtypeStruct((width, rows), F32),
            jax.ShapeDtypeStruct((width + 16, rows), BF16),
            jax.ShapeDtypeStruct((8, rows), F32),
        ],
        scratch_shapes=[
            pltpu.VMEM(x.shape, BF16),
            pltpu.VMEM(w_t.shape, BF16),
            pltpu.VMEM(gains.shape, F32),
            pltpu.SemaphoreType.DMA((2, 2)),
            pltpu.SemaphoreType.DMA,
        ],
        compiler_params=vmem_limit(24),
        cost_estimate=pl.CostEstimate(flops=2 * rows * feat * width, bytes_accessed=10_000_000, transcendentals=0),
    )(in_hbm(x), in_hbm(w_t), in_hbm(gains))


def head_kernel(
    model_width,
    where_ref,
    masks_ref,
    lens_ref,
    part_ref,
    got_ref,
    sq_ref,
    t_hbm,
    dest_ref,
    gain_ref,
    x_hbm,
    d_hbm,
    loss_ref,
    a_hbm,
    b_hbm,
    c_hbm,
    target_ref,
    x_ref,
    d_ref,
    a_ref,
    b_ref,
    c_ref,
    sems,
    out_sems,
):
    t_copy = pltpu.make_async_copy(t_hbm, target_ref, sems.at[0])
    x_copy = pltpu.make_async_copy(x_hbm, x_ref, sems.at[1])
    t_copy.start()
    x_copy.start()
    width, rows = part_ref.shape
    lat = gain_ref.shape[0]
    groups = lens_ref.shape[0]
    blk = d_ref.shape[1]
    trainers = loss_ref.shape[0]
    lanes = 256
    gain = gain_ref[...]
    sums = None
    t_copy.wait()
    for first in range(0, rows, lanes):
        cut = slice(first, first + lanes)
        terms = got_ref[width:, cut].astype(F32)
        squares = sq_ref[:1, cut] + (terms[0:1] + terms[1:2] + terms[2:3])
        scale = lax.rsqrt(squares / model_width + EPS)
        position = lax.broadcasted_iota(jnp.int32, (1, lanes), 1) + first
        length = jnp.zeros((1, lanes), jnp.int32)
        start = 0
        for g in range(groups):
            size = lens_ref[g]
            length = jnp.where((position >= start) & (position < start + size), size, length)
            start = start + size
        weight = (1.0 / length.astype(F32)).astype(BF16).astype(F32)

        comp = (part_ref[:lat, cut] + got_ref[:lat, cut].astype(F32)) * scale
        factor = lax.rsqrt(jnp.mean(comp * comp, axis=0, keepdims=True) + EPS)
        res_c = comp * factor * gain - target_ref[:lat, cut].astype(F32)
        res_r = (part_ref[lat:, cut] + got_ref[lat:width, cut].astype(F32)) * scale
        res_r = res_r - target_ref[lat:, cut].astype(F32)
        total = jnp.sum(res_c * res_c, axis=0, keepdims=True) + jnp.sum(res_r * res_r, axis=0, keepdims=True)
        row_terms = weight * (0.5 * (total / width)) / groups
        scaled = weight * res_c * gain
        inner = jnp.mean(scaled * comp, axis=0, keepdims=True)
        d_c = (factor * scale) * scaled - comp * (factor * factor * factor * inner * scale)
        d_r = (weight * scale) * res_r
        for j in range(d_ref.shape[0]):
            lo, hi = j * blk, (j + 1) * blk
            if hi <= lat:
                piece = d_c[lo:hi]
            elif lo >= lat:
                piece = d_r[lo - lat : hi - lat]
            else:
                piece = jnp.concatenate([d_c[lo:], d_r[: hi - lat]], axis=0)
            d_ref[(j // 4) * 4 + ((j % 4) ^ masks_ref[j // 4]), :, cut] = piece.astype(BF16)
        named = dest_ref[:, cut] == lax.broadcasted_iota(jnp.int32, (trainers, lanes), 0)
        named = jnp.where(named, row_terms, 0.0)
        for c in range(0, lanes, 128):
            sums = named[:, c : c + 128] if sums is None else sums + named[:, c : c + 128]
    loss_ref[...] = jnp.broadcast_to(jnp.sum(sums, axis=1, keepdims=True), loss_ref.shape)
    d_copy = pltpu.make_async_copy(d_ref, d_hbm, sems.at[2])
    d_copy.start()
    x_copy.wait()
    copies = []

    def send(chain, half, slot):
        near, away = (a_ref, b_ref, c_ref)[chain], (a_hbm, b_hbm, c_hbm)[chain]
        copies.append(pltpu.make_async_copy(near.at[half], away.at[slot], out_sems.at[chain, half]))
        copies[-1].start()

    grad_halves(where_ref, d_ref, x_ref, (a_ref, b_ref, c_ref), send)
    for copy in copies:
        copy.wait()
    d_copy.wait()


def grad_halves(where_ref, d_ref, x_ref, out_refs, send=None):
    blocks, blk, rows = d_ref.shape
    cols = out_refs[0].shape[-1]
    for first, count in ((2, 1), (0, 2)):
        lhs = d_ref[first * 4 : (first + count) * 4].reshape(count * 4 * blk, rows)
        for i in range(2):
            col = pl.multiple_of((where_ref[2 * first] * 2 + i) * cols, 128)
            out = jnp.dot(lhs, x_ref[:, pl.ds(col, cols)], preferred_element_type=F32).astype(BF16)
            for c in range(count):
                part = out[c * 4 * blk : (c + 1) * 4 * blk]
                slot = i ^ where_ref[2 * (first + c) + 1]
                out_refs[first + c][i if send else slot] = part.reshape(4, blk, cols)
                if send:
                    send(first + c, i, slot)


def head_call(part, got, sq, targets_t, dest_row, lengths, gain_col, x, where, row_masks, model_width, trainers):
    width, rows = part.shape
    blk, cols = width // 12, x.shape[1] // 4
    return pl.pallas_call(
        functools.partial(head_kernel, model_width),
        in_specs=[scalars()] * 3 + [whole()] * 3 + [far()] + [whole()] * 2 + [far()],
        out_specs=[far(), whole(), far(), far(), far()],
        out_shape=[
            pltpu.HBM((12, blk, rows), BF16),
            jax.ShapeDtypeStruct((trainers, 128), F32),
        ]
        + [pltpu.HBM((2, 4, blk, cols), BF16)] * 3,
        scratch_shapes=[
            pltpu.VMEM(targets_t.shape, BF16),
            pltpu.VMEM(x.shape, BF16),
            pltpu.VMEM((12, blk, rows), BF16),
        ]
        + [pltpu.VMEM((2, 4, blk, cols), BF16)] * 3
        + [
            pltpu.SemaphoreType.DMA((3,)),
            pltpu.SemaphoreType.DMA((3, 2)),
        ],
        compiler_params=vmem_limit(24),
        cost_estimate=pl.CostEstimate(flops=width * rows * cols * 4, bytes_accessed=12_000_000, transcendentals=0),
    )(where, row_masks, lengths, part, got, sq, in_hbm(targets_t), dest_row, gain_col, in_hbm(x))


def keep_kernel(where_ref, d_hbm, x_hbm, a_ref, b_ref, c_ref, d_ref, x_ref, sems):
    d_copy = pltpu.make_async_copy(d_hbm, d_ref, sems.at[0])
    x_copy = pltpu.make_async_copy(x_hbm, x_ref, sems.at[1])
    d_copy.start()
    x_copy.start()
    d_copy.wait()
    x_copy.wait()
    grad_halves(where_ref, d_ref, x_ref, (a_ref, b_ref, c_ref))


def keep_call(d, x, where):
    blk, cols = d.shape[1], x.shape[1] // 4
    return pl.pallas_call(
        keep_kernel,
        in_specs=[scalars(), far(), far()],
        out_specs=[whole()] * 3,
        out_shape=[jax.ShapeDtypeStruct((2, 4, blk, cols), BF16)] * 3,
        scratch_shapes=[pltpu.VMEM(d.shape, BF16), pltpu.VMEM(x.shape, BF16), pltpu.SemaphoreType.DMA((2,))],
        compiler_params=vmem_limit(24),
        cost_estimate=pl.CostEstimate(flops=12 * blk * d.shape[2] * cols * 4, bytes_accessed=10_000_000, transcendentals=0),
    )(where, in_hbm(d), in_hbm(x))


def w_copies(where_ref, w_hbm, w_buf, sem, count):
    rows, cols = w_buf.shape[1:]
    copies = []
    for s in range(count):
        chain = (s % 6) // 2
        col = pl.multiple_of(where_ref[s] * cols, 128)
        tile = w_hbm.at[pl.ds(chain * rows, rows), pl.ds(col, cols)]
        copies.append(pltpu.make_async_copy(tile, w_buf.at[s], sem.at[s]))
        copies[-1].start()
    return copies


def step_size(entries, mine_ref, other_ref):
    return RATE * lax.rsqrt((mine_ref[16:17] + other_ref[16:17]) / entries + EPS)


def factors(where_ref, coef, gain_ref, s, cols):
    return jnp.concatenate([coef] * (cols // 128), axis=1) * gain_slice(gain_ref, where_ref[s] * cols, cols)


def updated_block(factor, w_buf, g_ref, s, j, mask):
    blk, cols = g_ref.shape[2:]
    g = g_ref[s % 2, j ^ mask].astype(F32)
    return w_buf[s, j * blk : (j + 1) * blk].astype(F32) - factor * g


def top_kernel(entries, where_ref, sum_ref, sum2_ref, gain_ref, w_hbm, *rest):
    g_refs, (out_ref, w_buf, sem) = rest[:6], rest[6:]
    copies = w_copies(where_ref, w_hbm, w_buf, sem, 12)
    blk, cols = g_refs[0].shape[2:]
    coef = step_size(entries, sum_ref, sum2_ref)
    for s in range(12):
        chain = (s % 6) // 2
        factor = factors(where_ref, coef, gain_ref, s, cols)
        copies[s].wait()
        for j in range(4):
            g_ref = g_refs[3 * (s // 6) + chain]
            size = jnp.abs(updated_block(factor, w_buf, g_ref, s, j, where_ref[12 + chain]))
            here = slice((chain * 4 + j) * blk, (chain * 4 + j + 1) * blk)
            top = size[:, :128]
            for k in range(1, cols // 128):
                top = jnp.maximum(top, size[:, k * 128 : (k + 1) * 128])
            if s > 5 or s % 2 > 0:
                top = jnp.maximum(top, out_ref[here])
            out_ref[here] = top


def top_all(entries, pieces, w_t, gains, sums, columns, row_masks):
    blk, cols = pieces[0].shape[-2:]
    where = jnp.stack([*columns, *row_masks]).astype(jnp.int32)
    return pl.pallas_call(
        functools.partial(top_kernel, entries),
        in_specs=[scalars(), whole(), whole(), whole(), far()] + [whole()] * 6,
        out_specs=whole(),
        out_shape=jax.ShapeDtypeStruct((w_t.shape[0], 128), F32),
        scratch_shapes=[pltpu.VMEM((12, 4 * blk, cols), BF16), pltpu.SemaphoreType.DMA((12,))],
        compiler_params=vmem_limit(20),
        cost_estimate=pl.CostEstimate(flops=4 * w_t.size, bytes_accessed=4 * w_t.size, transcendentals=0),
    )(where, *sums, gains, in_hbm(w_t), *pieces)


def code_kernel(entries, where_ref, sum_ref, sum2_ref, gain_ref, w_hbm, mine_ref, other_ref, *rest):
    g_refs, (out_ref, buf, w_buf, inv_ref, sem, w_sem) = rest[:6], rest[6:]
    loads = w_copies(where_ref, w_hbm, w_buf, w_sem, 12)
    blk, cols = g_refs[0].shape[2:]
    rows = 4 * blk
    top = jnp.max(jnp.maximum(mine_ref[...], other_ref[...]), axis=1, keepdims=True)
    inv_ref[...] = jnp.broadcast_to(1.0 / (top + EPS), inv_ref.shape)
    coef = step_size(entries, sum_ref, sum2_ref)
    copies = []
    for s in range(12):
        chain = (s % 6) // 2
        g_ref = g_refs[3 * (s // 6) + chain]
        factor = factors(where_ref, coef, gain_ref, s, cols)
        loads[s].wait()
        for j in range(4):
            new = updated_block(factor, w_buf, g_ref, s, j, where_ref[12 + chain])
            first = chain * rows + j * blk
            inv = jnp.concatenate([inv_ref[first : first + blk]] * (cols // 128), axis=1)
            buf[s, j * blk : (j + 1) * blk] = (new * inv).astype(BF16)
        col = pl.multiple_of(where_ref[s] * cols, 128)
        tile = out_ref.at[pl.ds(chain * rows, rows), pl.ds(col, cols)]
        copies.append(pltpu.make_async_copy(buf.at[s], tile, sem.at[s]))
        copies[-1].start()
    for copy in copies:
        copy.wait()


def code_all(entries, pieces, w_t, gains, sums, mine, other, columns, row_masks):
    blk, cols = pieces[0].shape[-2:]
    where = jnp.stack([*columns, *row_masks]).astype(jnp.int32)
    return pl.pallas_call(
        functools.partial(code_kernel, entries),
        in_specs=[scalars(), whole(), whole(), whole(), far()] + [whole()] * 8,
        out_specs=far(),
        out_shape=jax.ShapeDtypeStruct(w_t.shape, BF16),
        scratch_shapes=[
            pltpu.VMEM((12, 4 * blk, cols), BF16),
            pltpu.VMEM((12, 4 * blk, cols), BF16),
            pltpu.VMEM((w_t.shape[0], 128), F32),
            pltpu.SemaphoreType.DMA((12,)),
            pltpu.SemaphoreType.DMA((12,)),
        ],
        compiler_params=vmem_limit(24),
        cost_estimate=pl.CostEstimate(flops=8 * w_t.size, bytes_accessed=6 * w_t.size, transcendentals=0),
    )(where, *sums, gains, in_hbm(w_t), mine, other, *pieces)


def paired_shards(hidden, targets, group_lengths, dest_ids, input_gain, latent_gain, kv_weight):
    rows, feat = hidden.shape
    width = kv_weight.shape[1]
    model_width = 2 * feat
    blk, cols = width // 12, feat // 4
    roll = lax.axis_index("roll")
    core = lax.axis_index("tp")
    x_bit, y_bit = roll & 1, (roll >> 1) & 1
    bit = {
        "xy": jnp.where(core == 0, x_bit, y_bit),
        "yx": jnp.where(core == 0, y_bit, x_bit),
        "lo": (roll >> 2) & 1,
        "hi": (roll >> 3) & 1,
    }
    bits = [[bit[step] for step in order] for order in SCATTER]
    row_masks = [b[2] * 2 + b[3] for b in bits]

    w_t = kv_weight.T
    gains = input_gain.reshape(feat // 128, 128)
    part, sent, squares = forward(hidden, w_t, gains)
    got = swap_cores(sent)
    give = jnp.stack([v for b in bits for v in (1 - b[0], b[1])]).astype(jnp.int32)
    take = jnp.stack([v for b in bits for v in (b[0], b[1])]).astype(jnp.int32)
    d, losses, *away = head_call(
        part,
        got,
        squares,
        targets.T,
        dest_ids.T,
        group_lengths[0],
        latent_gain[:, None],
        hidden,
        give,
        jnp.stack(row_masks).astype(jnp.int32),
        model_width,
        16,
    )
    held = keep_call(d, hidden, take)
    own_cols = [b[0] * 2 + b[1] for b in bits]
    own_gain = [lax.dynamic_slice(input_gain, (c * cols,), (cols,)) for c in own_cols]
    shape = (1, 2, 2, 2, blk, cols)
    away = [v.reshape(shape) for v in away]
    held = [v.reshape(shape) for v in held]
    taken = [0] * 4
    flight = [None] * 4
    sums = [None] * 3
    settled = []
    small = None
    for lane in PLAN:
        step, taken[lane] = divmod(taken[lane], 2)[0], taken[lane] + 1
        if flight[lane] is None:
            if lane == 3:
                if step == 0:
                    power = sum(jnp.sum(jnp.square(v.astype(F32) * g)) for v, g in zip(sums, own_gain))
                    small = jnp.concatenate([0.5 * losses, jnp.broadcast_to(power, (8, 128))], axis=0)
                message = small
            elif step == 0:
                message = away[lane]
            elif step < 4:
                message = lax.index_in_dim(held[lane], 1, step, keepdims=True)
            else:
                message = held[lane]
            if settled:
                message, *_ = lax.optimization_barrier((message, *settled))
                settled = []
            if lane == 3:
                flight[lane] = exchange(message, SMALL[step]) if step < 4 else swap_cores(message)
            else:
                order = SCATTER[lane]
                flight[lane] = exchange(message, order[step] if step < 4 else order[GATHER[lane][step - 4]])
            continue
        got, flight[lane] = flight[lane], None
        if lane == 3:
            if step == 4:
                both = (small, got)
            else:
                small = small + got
                settled.append(small)
        elif step < 4:
            keep = held[lane] if step == 0 else lax.index_in_dim(held[lane], 0, step, keepdims=True)
            held[lane] = sums[lane] = add(keep, got)
            settled.append(held[lane])
        elif step < 7:
            held[lane] = jnp.concatenate([held[lane], got], axis=GATHER[lane][step - 4])
            settled.append(held[lane])
        else:
            held[lane] = (held[lane], got)

    entries = model_width * width
    pieces, columns = [], []
    for n in range(2):
        part = [held[chain][n].reshape(2, 4, blk, cols) for chain in range(3)]
        spots = []
        for chain in range(3):
            inner = GATHER[chain][3] == 1
            spots += [(2 * i + n if inner else 2 * n + i) ^ own_cols[chain] for i in range(2)]
        pieces += part
        columns += spots
    top = top_all(entries, pieces, w_t, gains, both, columns, row_masks)
    codes = code_all(entries, pieces, w_t, gains, both, top, swap_cores(top), columns, row_masks)
    loss = sum(lax.dynamic_slice(v, (roll, 0), (1, 1)) for v in both)
    return loss.reshape(1), codes.T


def any_shards(hidden, targets, group_lengths, dest_ids, input_gain, latent_gain, kv_weight):
    rows, feat = hidden.shape
    width = kv_weight.shape[1]
    roll_count = lax.axis_size("roll")
    model_width = feat * lax.axis_size("tp")
    wide = hidden.astype(F32)
    scale = lax.rsqrt(lax.psum(jnp.sum(wide * wide, axis=1), "tp") / model_width + EPS)
    normed = (wide * scale[:, None] * input_gain).astype(BF16)
    latent = lax.psum(jnp.dot(normed, kv_weight, preferred_element_type=F32), "tp")
    weights = row_weights(group_lengths[0], rows)
    row_terms, d_latent = head(latent.T, targets.T, weights, latent_gain, group_lengths.shape[1])
    grad = lax.dot_general(
        d_latent.astype(BF16), normed, (((1,), (0,)), ((), ())), preferred_element_type=F32
    )
    grad = lax.psum(grad.astype(BF16), "roll").astype(F32)
    dest = dest_ids[:, 0]
    named = dest[None, :] == lax.iota(jnp.int32, roll_count)[:, None]
    losses = lax.psum(jnp.sum(jnp.where(named, row_terms[None, :], 0.0), axis=1), "roll")
    power = lax.psum(jnp.sum(grad * grad), "tp")
    updated = kv_weight.T.astype(F32) - RATE * grad * lax.rsqrt(power / (model_width * width) + EPS)
    peak = lax.pmax(jnp.max(jnp.abs(updated), axis=1), "tp") + EPS
    codes = (updated / peak[:, None]).astype(BF16)
    loss = lax.dynamic_slice(losses, (lax.axis_index("roll"),), (1,))
    return loss, codes.T


def solution(mesh):
    in_specs = (
        P("roll", "tp"),
        P("roll", None),
        P("roll", None),
        P("roll", None),
        P("tp"),
        P(),
        P("tp", None),
    )
    out_specs = (P("roll"), P("tp", None))
    paired = mesh.shape["roll"] == 16 and mesh.shape["tp"] == 2
    body = paired_shards if paired else any_shards
    return jax.shard_map(body, mesh=mesh, in_specs=in_specs, out_specs=out_specs, check_vma=False)
```
